32 devices in a mesh: seq: 16 (over z, y, core), head: 2 (over x).
Axes of the slice: x: 2, y: 2, z: 4, core: 2. Of those that a mesh axis runs over, the one named last changes fastest.
Arguments:
- queries: bfloat16 [4096, 2048], P(('seq', 'head')), may hold values from -28 to 28
- key_states: bfloat16 [4096, 512], P(('seq', 'head')), may hold values from -20 to 20
- value_vector_rows: bfloat16 [4096, 512], P(('seq', 'head')), may hold values from -6 to 6
- grad_output: bfloat16 [4096, 2048], P(('seq', 'head')), may hold values from -6 to 6
- doc_ids: int32 [32], replicated, may hold values from 0 to 3, never falling along the last dimension, each value on 1 to 16 neighbouring positions
- block_home: int32 [32], replicated, may hold values from 0 to 31, as said below
Outputs:
- attended: bfloat16 [4096, 2048], P('seq', 'head')
- grad_query: bfloat16 [4096, 2048], P('seq', 'head')
- key_gradient: bfloat16 [4096, 512], P('seq', 'head')
- value_gradient: bfloat16 [4096, 512], P('seq', 'head')
The draws below stay inside these ranges and needn't reach their ends.
Inputs may be any that keep to these rules, and one draw needn't show every extreme that they name: `block_home`: a permutation of the natural blocks; slots are numbered shard by shard, 2 slots to a seq shard; every block sits in its natural shard (block // 2) or one beside it, and across each boundary between neighbouring shards exactly one block moves each way.
All inputs are finite; a program needn't handle non-finite values.
Results may differ from the reference program's by a relative error of at most 0.025.
Values may be sent and summed in bfloat16 or wider, within the bound.
No kernel may reach another device: no remote copies, remote signals or barrier semaphores. Data moves between devices by JAX's collectives and lax.ppermute only.
A program may use at most 192 MiB of HBM per device.

```python
import math
import jax
import jax.numpy as jnp
import numpy as np
from jax import lax

TOKENS_PER_PART = 256
BLK = 128
WINDOW = 2048
QUERY_HEADS = 16
KEY_VALUE_HEADS = 4
HEAD_SIZE = 128
CONTEXT_TOKENS = 4096
NBLOCKS = 32
N_SEQ = 16


def shared_base(key):
    gaussian_sample = jax.random.normal(jax.random.fold_in(key, 101), (CONTEXT_TOKENS, KEY_VALUE_HEADS * HEAD_SIZE), jnp.float32)
    return jnp.clip(gaussian_sample, -4.0, 4.0)


def draw_key_states(key, part):
    lowest_offset = shared_base(key)
    return lowest_offset.astype(jnp.bfloat16)


def draw_queries(key, part):
    own_draw = jnp.clip(jax.random.normal(jax.random.fold_in(key, 202), (CONTEXT_TOKENS, QUERY_HEADS * HEAD_SIZE), jnp.float32), -4.0, 4.0)
    return own_draw.astype(jnp.bfloat16)


def draw_block_home(key, part):
    block_count = TOKENS_PER_PART // BLK
    shard_total = NBLOCKS // block_count
    boundary = jnp.arange(shard_total, dtype=jnp.int32)
    flips = (boundary < shard_total - 1).astype(jnp.int32)
    earlier = jnp.concatenate([jnp.zeros((1,), jnp.int32), flips[:-1]])
    slot_index = jnp.arange(NBLOCKS, dtype=jnp.int32)
    shard_of = slot_index // block_count
    within = slot_index % block_count
    home = slot_index + jnp.where(within == block_count - 1, flips[shard_of], 0) - jnp.where(within == 0, earlier[shard_of], 0)
    turns = jax.random.randint(jax.random.fold_in(key, 12), (shard_total,), 0, block_count).astype(jnp.int32)
    source = shard_of * block_count + (within + turns[shard_of]) % block_count
    return home[source].astype(jnp.int32)


def block_scale(rng, dims, pieces, low, high):
    def one(dim, parts):
        heights = jax.random.uniform(jax.random.fold_in(jax.random.fold_in(rng, 6), dim), (parts,), jnp.float32, low / len(pieces), high / len(pieces))
        return jnp.repeat(jnp.exp(heights), dims[dim] // parts).reshape((-1,) + (1,) * (len(dims) - dim - 1))

    level = one(*pieces[0])
    for cut in pieces[1:]:
        level = level * one(*cut)
    return level


def profile(amount, total, bound, lean):
    weights = [(1 << 20) // math.isqrt(grade ** lean) + 1 for grade in range(2, amount + 1)]
    spare, counts = total - bound - (amount - 1), [1] * (amount - 1)
    while spare > 0:
        free = [i for i in range(amount - 1) if counts[i] < bound]
        whole, budget = sum([weights[i] for i in free]), spare
        for i in free:
            addition = min(bound - counts[i], max(1, budget * weights[i] // whole), spare)
            counts[i] = counts[i] + addition
            spare = spare - addition
    return np.array([bound] + counts)


def ragged(own_key, count, total, bound, slope):
    if count == 2:
        one = jax.random.randint(own_key, (), max(1, total - bound), min(bound, total - 1) + 1)
        return jnp.stack([one, total - one])
    sizes = jnp.asarray(profile(count, total, bound, slope), jnp.int32)
    twos = (count - 1) // 2
    source_of, receiver = sizes[1:1 + 2 * twos:2], sizes[2:2 + 2 * twos:2]
    room = jnp.minimum(source_of - 1, bound - receiver)
    passed = jax.random.randint(jax.random.fold_in(own_key, 1), (twos,), 0, 1 << 20) % (room + 1)
    sizes = sizes.at[1:1 + 2 * twos:2].set(source_of - passed).at[2:2 + 2 * twos:2].set(receiver + passed)
    return sizes[jax.random.permutation(jax.random.fold_in(own_key, 2), count)]


def noise(key, extent, spread, bound, cuts=(), held_as=jnp.bfloat16):
    array = spread * jax.random.normal(key, extent, jnp.float32)
    if cuts:
        array = array * block_scale(key, extent, cuts, -0.22, 0.18)
    return jnp.clip(array, -bound, bound).astype(held_as)


def setup_inputs(seed: int = 0) -> dict:
    seeds = jax.random.split(jax.random.key(seed), 7)
    queries = draw_queries(jax.random.fold_in(seeds[6], 71), 0)
    key_states = draw_key_states(jax.random.fold_in(seeds[6], 71), 0)
    value_vector_rows = noise(seeds[2], (CONTEXT_TOKENS, KEY_VALUE_HEADS * HEAD_SIZE), 1.0, 6.0, ((0, 32),))
    grad_output = noise(seeds[3], (CONTEXT_TOKENS, QUERY_HEADS * HEAD_SIZE), 1.0, 6.0, ((0, 32),))
    doc_ids = jnp.searchsorted(jnp.cumsum(ragged(seeds[4], NBLOCKS // 8, NBLOCKS, min(64, NBLOCKS // 2), 2)), jnp.arange(NBLOCKS), side="right").astype(jnp.int32)
    block_home = draw_block_home(jax.random.fold_in(seeds[6], 71), 0)
    return dict(queries=queries, key_states=key_states, value_vector_rows=value_vector_rows, grad_output=grad_output, doc_ids=doc_ids, block_home=block_home)


def reference(queries, key_states, value_vector_rows, grad_output, doc_ids, block_home):
    block_count = TOKENS_PER_PART // BLK
    reach = WINDOW // TOKENS_PER_PART
    queries_per_group = QUERY_HEADS // KEY_VALUE_HEADS
    reciprocal_root = 1.0 / math.sqrt(HEAD_SIZE)
    listing = jnp.arange(NBLOCKS, dtype=jnp.int32)
    inverse = jnp.zeros((NBLOCKS,), jnp.int32).at[block_home].set(listing)

    def natural(source):
        return source.reshape(NBLOCKS, BLK, source.shape[1])[inverse].reshape(CONTEXT_TOKENS, source.shape[1])
    query_natural_order = natural(queries)
    key_natural_order = natural(key_states)
    value_natural_order = natural(value_vector_rows)
    gradient_natural_order = natural(grad_output)
    filler_rows = reach * TOKENS_PER_PART
    reach_extent = filler_rows + TOKENS_PER_PART
    key_padded = jnp.concatenate([jnp.zeros((filler_rows, KEY_VALUE_HEADS * HEAD_SIZE), jnp.bfloat16), key_natural_order], axis=0)
    value_padded = jnp.concatenate([jnp.zeros((filler_rows, KEY_VALUE_HEADS * HEAD_SIZE), jnp.bfloat16), value_natural_order], axis=0)
    doc_tok = jnp.repeat(doc_ids, BLK)
    doc_pad = jnp.concatenate([jnp.full((filler_rows,), -1, jnp.int32), doc_tok])
    row_index = jnp.arange(TOKENS_PER_PART, dtype=jnp.int32)
    col_index = jnp.arange(reach_extent, dtype=jnp.int32)
    top_precision = lax.Precision.HIGHEST

    def shard_step(running_total, shard):
        begin_offset = (shard * TOKENS_PER_PART).astype(jnp.int32)
        local_query = lax.dynamic_slice_in_dim(query_natural_order, begin_offset, TOKENS_PER_PART, 0).reshape(TOKENS_PER_PART, KEY_VALUE_HEADS, queries_per_group, HEAD_SIZE).astype(jnp.float32)
        gradient_local = lax.dynamic_slice_in_dim(gradient_natural_order, begin_offset, TOKENS_PER_PART, 0).reshape(TOKENS_PER_PART, KEY_VALUE_HEADS, queries_per_group, HEAD_SIZE).astype(jnp.float32)
        local_keys = lax.dynamic_slice_in_dim(key_padded, begin_offset, reach_extent, 0).reshape(reach_extent, KEY_VALUE_HEADS, HEAD_SIZE).astype(jnp.float32)
        local_values = lax.dynamic_slice_in_dim(value_padded, begin_offset, reach_extent, 0).reshape(reach_extent, KEY_VALUE_HEADS, HEAD_SIZE).astype(jnp.float32)
        query_doc = lax.dynamic_slice_in_dim(doc_tok, begin_offset, TOKENS_PER_PART, 0)
        key_doc = lax.dynamic_slice_in_dim(doc_pad, begin_offset, reach_extent, 0)
        distance = row_index[:, None] + filler_rows - col_index[None, :]
        visible = (query_doc[:, None] == key_doc[None, :]) & (distance >= 0) & (distance < WINDOW)
        scores = jnp.einsum('tgqd,ugd->gqtu', local_query, local_keys, precision=top_precision) * reciprocal_root
        row_max = lax.optimization_barrier(jnp.max(jnp.where(visible, scores, -1e+30), axis=-1, keepdims=True))
        row_sum = lax.optimization_barrier(jnp.sum(jnp.where(visible, jnp.exp(scores - row_max), 0.0), axis=-1, keepdims=True))
        log_total = row_max + jnp.log(row_sum)
        prob = jnp.where(visible, jnp.exp(scores - log_total), 0.0)
        probability_lowered = lax.optimization_barrier(prob.astype(jnp.bfloat16)).astype(jnp.float32)
        attended = jnp.einsum('gqtu,ugd->tgqd', probability_lowered, local_values, precision=top_precision).astype(jnp.bfloat16)
        delta = jnp.transpose(lax.optimization_barrier(jnp.sum(gradient_local * attended.astype(jnp.float32), axis=-1)), (1, 2, 0))
        grad_prob = jnp.einsum('tgqd,ugd->gqtu', gradient_local, local_values, precision=top_precision)
        score_gradient = lax.optimization_barrier((prob * (grad_prob - delta[..., None])).astype(jnp.bfloat16)).astype(jnp.float32)
        grad_query = (jnp.einsum('gqtu,ugd->tgqd', score_gradient, local_keys, precision=top_precision) * reciprocal_root).astype(jnp.bfloat16)
        key_contribution = jnp.einsum('nzev,enzx->vnx', score_gradient, local_query, precision=top_precision).reshape(reach_extent, KEY_VALUE_HEADS * HEAD_SIZE)
        value_contribution = jnp.einsum('nzev,enzx->vnx', probability_lowered, gradient_local, precision=top_precision).reshape(reach_extent, KEY_VALUE_HEADS * HEAD_SIZE)
        shard_term = jnp.concatenate([key_contribution, value_contribution], axis=1)
        old = lax.dynamic_slice_in_dim(running_total, begin_offset, reach_extent, 0)
        running_total = lax.dynamic_update_slice_in_dim(running_total, old + shard_term, begin_offset, 0)
        return (running_total, (attended.reshape(TOKENS_PER_PART, QUERY_HEADS * HEAD_SIZE), grad_query.reshape(TOKENS_PER_PART, QUERY_HEADS * HEAD_SIZE)))
    running_begin = jnp.zeros((filler_rows + CONTEXT_TOKENS, 2 * KEY_VALUE_HEADS * HEAD_SIZE), jnp.float32)
    running_total, stacked = lax.scan(shard_step, running_begin, jnp.arange(N_SEQ, dtype=jnp.int32))
    attended_all = stacked[0].reshape(CONTEXT_TOKENS, QUERY_HEADS * HEAD_SIZE)
    grad_query_all = stacked[1].reshape(CONTEXT_TOKENS, QUERY_HEADS * HEAD_SIZE)
    key_gradient = (running_total[filler_rows:, :KEY_VALUE_HEADS * HEAD_SIZE] * reciprocal_root).astype(jnp.bfloat16)
    value_gradient = running_total[filler_rows:, KEY_VALUE_HEADS * HEAD_SIZE:].astype(jnp.bfloat16)
    return (attended_all, grad_query_all, key_gradient, value_gradient)
```

```python
import functools
import math

import jax
import jax.numpy as jnp
from jax import lax
from jax.experimental import pallas as pl
from jax.experimental.pallas import tpu as pltpu
from jax.sharding import PartitionSpec as P

BLK = 128
WINDOW = 2048
HEAD = 128
ROOT = 1.0 / math.sqrt(HEAD)
EXP2_SCALE = ROOT * math.log2(math.e)
HIDDEN = -1e30
NN = (((1,), (0,)), ((), ()))
TN = (((0,), (0,)), ((), ()))
SAFE_TOTAL = 2.0**60
SIDES = 2
BACK = 4
CHUNKS = SIDES * (BACK + 1)
SPLIT = 2 * SIDES
FLIPS = ((0, 0), (0, 1), (1, 0), (1, 1))
VMEM = pl.BlockSpec(memory_space=pltpu.VMEM)
SMEM = pl.BlockSpec(memory_space=pltpu.SMEM)
ANY = pl.BlockSpec(memory_space=pl.ANY)
SMALL = pltpu.CompilerParams(vmem_limit_bytes=8 * 1024 * 1024)
def dot(a, b, dims):
    return lax.dot_general(a, b, dims, preferred_element_type=jnp.float32)


def position():
    seq_at = lax.axis_index("seq")
    return seq_at // SIDES, seq_at % SIDES, lax.axis_index("head")


def local_slots(chip_at, core_at, head_at):
    return [
        SIDES * 2 * chip_at + 2 * (core_at ^ core_flip) + (head_at ^ head_flip)
        for core_flip, head_flip in FLIPS
    ]


def turned(array):
    return jnp.transpose(array.astype(jnp.float32))


def pack_kernel(width, one, two, p0, p1, p2, p3, landed, sems):
    copies = [
        pltpu.make_async_copy(ref, landed.at[which], sems.at[which])
        for which, ref in enumerate((one, two))
    ]
    for copy in copies:
        copy.start()
    for copy in copies:
        copy.wait()
    unused, core_at, head_at = position()
    for target, (core_flip, head_flip) in zip((p0, p1, p2, p3), FLIPS):
        group = SIDES * (head_at ^ head_flip) + (core_at ^ core_flip)
        columns = pl.ds(pl.multiple_of(group * width, width), width)
        for which in range(2):
            target[:, which * width : (which + 1) * width] = landed[which, :, columns]


def pack(one, two, groups):
    rows, columns = one.shape
    width = columns // groups
    packet = jax.ShapeDtypeStruct((rows, 2 * width), jnp.bfloat16)
    return pl.pallas_call(
        functools.partial(pack_kernel, width),
        out_shape=[packet] * 4,
        in_specs=[ANY] * 2,
        out_specs=[VMEM] * 4,
        scratch_shapes=[
            pltpu.VMEM((2, rows, columns), jnp.bfloat16),
            pltpu.SemaphoreType.DMA((2,)),
        ],
        compiler_params=SMALL,
        cost_estimate=pl.CostEstimate(flops=0, bytes_accessed=8 * rows * columns, transcendentals=0),
    )(one, two)


def move_kernel(home, q0, q1, q2, q3, k0, k1, k2, k3, right, left):
    chip_at, core_at, head_at = position()
    width = q0.shape[1]
    for slot, q, k in zip(local_slots(chip_at, core_at, head_at), (q0, q1, q2, q3), (k0, k1, k2, k3)):
        target = home[slot] // (2 * SIDES)

        @pl.when(target > chip_at)
        def _():
            right[...] = q[...]

        @pl.when(target < chip_at)
        def _():
            left[:, :width] = q[...]
            left[:, width:] = k[...]


def movers(home, queries, keys):
    rows, width = queries[0].shape
    return pl.pallas_call(
        move_kernel,
        out_shape=[
            jax.ShapeDtypeStruct((rows, width), jnp.bfloat16),
            jax.ShapeDtypeStruct((rows, width + keys[0].shape[1]), jnp.bfloat16),
        ],
        in_specs=[SMEM] + [VMEM] * 8,
        out_specs=[VMEM] * 2,
        compiler_params=SMALL,
        cost_estimate=pl.CostEstimate(flops=0, bytes_accessed=8 * rows * width, transcendentals=0),
    )(home, *queries, *keys)


def end_kernel(home, k0, k1, k2, k3, right):
    chip_at, core_at, head_at = position()
    for slot, ref in zip(local_slots(chip_at, core_at, head_at), (k0, k1, k2, k3)):
        @pl.when(home[slot] // (2 * SIDES) > chip_at)
        def _():
            right[...] = ref[...]


def key_mover(home, keys):
    return pl.pallas_call(
        end_kernel,
        out_shape=jax.ShapeDtypeStruct(keys[0].shape, jnp.bfloat16),
        in_specs=[SMEM] + [VMEM] * 4,
        out_specs=VMEM,
        compiler_params=SMALL,
        cost_estimate=pl.CostEstimate(
            flops=0, bytes_accessed=8 * keys[0].size, transcendentals=0
        ),
    )(home, *keys)


def block_sources(home, chip_at, core_at, head_at, b):
    slots = local_slots(chip_at, core_at, head_at)
    before = jnp.maximum(2 * SIDES * (chip_at - 1), 0)
    block = 2 * SIDES * chip_at + b
    here = [home[slot] == block for slot in slots]
    from_left = home[before] == block
    for other in range(1, 2 * SIDES):
        from_left = from_left | (home[before + other] == block)
    outside = jnp.logical_not(here[0] | here[1] | here[2] | here[3])
    return here + [outside & from_left, outside & jnp.logical_not(from_left)]


def key_ranges(docs, chip_at):
    first = SIDES * (chip_at - BACK)

    def doc_at(j, half):
        return docs[jnp.maximum(2 * (first + j) + half, 0)]

    limit = [SIDES * BACK + i + 1 for i in range(SIDES)]
    lowest = []
    for i in range(SIDES):
        own = SIDES * BACK + i
        low = jnp.int32(own)
        for j in range(i, own):
            alike = (first + j >= 0) & (doc_at(j, 1) == doc_at(own, 0))
            low = low - alike.astype(jnp.int32)
        lowest.append(low)
    return doc_at, lowest, limit, jnp.minimum(lowest[0], lowest[1])


def gradient_loop(
    per_group, tokens, lowest, limit, start, stop, outputs,
    kv, values_turned, e_low, spread, q_stack, do_stack, dq, ds_low,
):
    def chunk(j):
        return pl.ds(pl.multiple_of(j * tokens, tokens), tokens)

    def store(j, value):
        for back, ref in outputs.items():
            @pl.when(j // SIDES == BACK - back)
            def _():
                ref[j % SIDES] = value

    def grad_terms(i, j):
        value_term = dot(e_low[i, j - i], do_stack[i], TN)
        key_term = None
        for h in range(per_group):
            rows = slice(h * tokens, (h + 1) * tokens)
            delta = spread[i, rows]
            dp = dot(do_stack[i, rows], values_turned[j], NN)
            e = e_low[i, j - i, rows].astype(jnp.float32)
            g0 = e[:, :HEAD] * (dp[:, :HEAD] - delta)
            g1 = e[:, HEAD:] * (dp[:, HEAD:] - delta)
            ds = jnp.concatenate([g0, g1], axis=1).astype(jnp.bfloat16)
            ds_low[i, rows] = ds
            dq[i, rows] += dot(ds, kv[chunk(j), :HEAD], NN)
            if h % 2 == 1:
                part = slice((h - 1) * tokens, (h + 1) * tokens)
                term = dot(ds_low[i, part], q_stack[i, part], TN)
                key_term = term if key_term is None else key_term + term
        return jnp.concatenate([key_term * ROOT, value_term], axis=1)

    def grad_pass(j, carry):
        inside = [(j >= lowest[i]) & (j < limit[i]) for i in range(SIDES)]

        @pl.when(inside[0] & inside[1])
        def _():
            store(j, (grad_terms(0, j) + grad_terms(1, j)).astype(jnp.bfloat16))

        for i in range(SIDES):
            @pl.when(inside[i] & jnp.logical_not(inside[1 - i]))
            def _():
                store(j, grad_terms(i, j).astype(jnp.bfloat16))

        return carry

    def no_terms(j, carry):
        store(j, jnp.zeros((tokens, 2 * HEAD), jnp.bfloat16))
        return carry

    begin = jnp.clip(jnp.minimum(lowest[0], lowest[1]), start, stop)
    lax.fori_loop(start, begin, no_terms, 0)
    lax.fori_loop(begin, stop, grad_pass, 0)


def attention_kernel(
    per_group, tokens, shards,
    docs, home, b0, b1, b2, b3, b4, b5, c0, c1, c2, c3, c4, end_far,
    keep, send, d3, d4, kv, values_turned, e_low, spread, q_stack, do_stack, dq,
    ones, keys_turned, top, acc, ds_low, landed, end_near, sems,
):
    chip_at, core_at, head_at = position()
    q_width = per_group * HEAD

    def land(ref, b):
        return pltpu.make_async_copy(ref.at[:, pl.ds(0, 2 * q_width)], landed.at[b], sems.at[b])

    end_copy = pltpu.make_async_copy(
        b5.at[:, pl.ds(2 * q_width, 2 * HEAD)], end_near, sems.at[2 * SIDES]
    )
    end_copy.start()

    for b in range(2 * SIDES):
        flags = block_sources(home, chip_at, core_at, head_at, b)
        for flag, ref in zip(flags, (b0, b1, b2, b3, b4, b5)):
            @pl.when(flag)
            def _():
                land(ref, b).start()

    chip_blocks = 2 * SIDES
    window = chip_blocks * (chip_at - BACK)

    def write_key_block(block, known, value):
        place = block - window

        @pl.when(known & (place >= 0) & (place < chip_blocks * (BACK + 1)))
        def _():
            rows = pl.ds(pl.multiple_of(place * BLK, BLK), BLK)
            kv[rows] = value[...]
            ones[rows, :HEAD] = value[:, HEAD:]
            ones[rows, HEAD:] = jnp.ones((BLK, HEAD), jnp.bfloat16)

    def write_chip(back, ref):
        known = chip_at >= back
        for which, slot in enumerate(local_slots(chip_at - back, core_at, head_at)):
            write_key_block(home[jnp.maximum(slot, 0)], known, ref.at[which])

    def write_end(chip, target, ref):
        known = (chip >= 0) & (chip < shards // SIDES)
        slot = jnp.where(known, chip_blocks * chip, 0)
        for other in range(chip_blocks):
            block = home[slot + other]
            write_key_block(block, known & (block // chip_blocks == target), ref)

    for back, ref in enumerate((c0, c1, c2, c3, c4)):
        write_chip(back, ref)
    write_end(chip_at - BACK - 1, chip_at - BACK, end_far)
    end_copy.wait()
    write_end(chip_at + 1, chip_at, end_near)
    for b in range(2 * SIDES):
        land(b0, b).wait()
        for h in range(per_group):
            rows = slice(h * tokens + (b % 2) * BLK, h * tokens + (b % 2 + 1) * BLK)
            q_stack[b // 2, rows] = landed[b, :, h * HEAD : (h + 1) * HEAD]
            do_stack[b // 2, rows] = landed[b, :, q_width + h * HEAD : q_width + (h + 1) * HEAD]

    def chunk(j):
        return pl.ds(pl.multiple_of(j * tokens, tokens), tokens)

    doc_at, lowest, limit, begin = key_ranges(docs, chip_at)

    row = lax.broadcasted_iota(jnp.int32, (tokens, tokens), 0)
    col = lax.broadcasted_iota(jnp.int32, (tokens, tokens), 1)

    def hidden(i, j):
        own = SIDES * BACK + i
        q_doc = jnp.where(row < BLK, doc_at(own, 0), doc_at(own, 1))
        k_doc = jnp.where(col < BLK, doc_at(j, 0), doc_at(j, 1))
        gap = row - col + (own - j) * tokens
        seen = (q_doc == k_doc) & (gap >= 0) & (gap < WINDOW)
        return jnp.where(seen, 0.0, HIDDEN)

    k_cols = slice(0, HEAD)
    v_cols = slice(HEAD, 2 * HEAD)

    def turn_chunk(j, carry):
        keys_turned[j] = turned(kv[chunk(j), k_cols]).astype(jnp.bfloat16)
        values_turned[j] = turned(kv[chunk(j), v_cols]).astype(jnp.bfloat16)
        return carry

    lax.fori_loop(begin, CHUNKS, turn_chunk, 0)

    def head_rows(h):
        return slice(h * tokens, (h + 1) * tokens)

    def in_range(i, j):
        return (j >= lowest[i]) & (j < limit[i])

    def is_open(i, j):
        own = SIDES * BACK + i
        return (
            in_range(i, j)
            & (doc_at(j, 0) == doc_at(own, 1))
            & (j < own)
            & (j > own - SIDES * BACK)
        )

    def take_top(i, start):
        top[i] = jnp.full_like(top[i], HIDDEN)

        def widen(j, carry):
            bias = hidden(i, j)
            for h in range(per_group):
                rows = head_rows(h)
                s = dot(q_stack[i, rows], keys_turned[j], NN) + bias
                top[i, rows] = jnp.maximum(top[i, rows], jnp.maximum(s[:, :HEAD], s[:, HEAD:]))
            return carry

        lax.fori_loop(start, limit[i], widen, 0)
        for h in range(per_group):
            rows = head_rows(h)
            top[i, rows] = jnp.broadcast_to(
                jnp.max(top[i, rows], axis=1, keepdims=True), (tokens, HEAD)
            )

    def forward(i, j, bias):
        for h in range(per_group):
            rows = head_rows(h)
            s = dot(q_stack[i, rows], keys_turned[j], NN)
            if bias is not None:
                s = s + bias
            m = top[i, rows]
            e0 = jnp.exp2((s[:, :HEAD] - m) * EXP2_SCALE)
            e1 = jnp.exp2((s[:, HEAD:] - m) * EXP2_SCALE)
            low = jnp.concatenate([e0, e1], axis=1).astype(jnp.bfloat16)
            e_low[i, j - i, rows] = low
            acc[i, rows] += dot(low, ones[chunk(j)], NN)

    def forward_pass(j, carry):
        open_all = is_open(0, j) & is_open(1, j)

        @pl.when(open_all)
        def _():
            for i in range(SIDES):
                forward(i, j, None)

        for i in range(SIDES):
            @pl.when(in_range(i, j) & jnp.logical_not(open_all))
            def _():
                forward(i, j, hidden(i, j))

        return carry

    def attempt(carry):
        tries, unused = carry
        for i in range(SIDES):
            take_top(i, jnp.where(tries == 0, SIDES * BACK + i, lowest[i]))
        acc[...] = jnp.zeros_like(acc)
        lax.fori_loop(begin, CHUNKS, forward_pass, 0)
        safe = jnp.min(jnp.where(acc[:, :, HEAD:] < SAFE_TOTAL, 1.0, 0.0))
        return tries + 1, (safe < 0.5).astype(jnp.int32)

    lax.while_loop(
        lambda carry: (carry[0] == 0) | ((carry[0] == 1) & (carry[1] == 1)),
        attempt,
        (jnp.int32(0), jnp.int32(0)),
    )

    for i in range(SIDES):
        for h in range(per_group):
            rows = head_rows(h)
            inverse = 1.0 / acc[i, rows, HEAD:]
            attended = (acc[i, rows, :HEAD] * inverse).astype(jnp.bfloat16)

            @pl.when(core_at == i)
            def _():
                keep[:, h * HEAD : (h + 1) * HEAD] = attended

            @pl.when(core_at != i)
            def _():
                send[:, h * HEAD : (h + 1) * HEAD] = attended

            shared = (do_stack[i, rows].astype(jnp.float32) * inverse).astype(jnp.bfloat16)
            do_stack[i, rows] = shared
            delta = jnp.sum(
                shared.astype(jnp.float32) * attended.astype(jnp.float32), axis=1, keepdims=True
            )
            spread[i, rows] = jnp.broadcast_to(delta, (tokens, HEAD))
    dq[...] = jnp.zeros_like(dq)

    gradient_loop(
        per_group, tokens, lowest, limit, 0, SPLIT, {3: d3, 4: d4},
        kv, values_turned, e_low, spread, q_stack, do_stack, dq, ds_low,
    )


def second_kernel(
    per_group, tokens,
    docs, kv, values_turned, e_low, spread, q_stack, do_stack, dq_first,
    keep, send, d0, d1, d2, dq, ds_low,
):
    chip_at, core_at, head_at = position()
    unused, lowest, limit, begin = key_ranges(docs, chip_at)
    dq[...] = dq_first[...]
    gradient_loop(
        per_group, tokens, lowest, limit, SPLIT, CHUNKS, {0: d0, 1: d1, 2: d2},
        kv, values_turned, e_low, spread, q_stack, do_stack, dq, ds_low,
    )
    for i in range(SIDES):
        for h in range(per_group):
            gradient = (dq[i, h * tokens : (h + 1) * tokens] * ROOT).astype(jnp.bfloat16)

            @pl.when(core_at == i)
            def _():
                keep[:, h * HEAD : (h + 1) * HEAD] = gradient

            @pl.when(core_at != i)
            def _():
                send[:, h * HEAD : (h + 1) * HEAD] = gradient


def per_device(queries, key_states, value_vector_rows, grad_output, doc_ids, block_home):
    seq_at = lax.axis_index("seq")
    shards = lax.axis_size("seq")
    heads = lax.axis_size("head")
    tokens = queries.shape[0] * heads
    groups = key_states.shape[1] // HEAD
    per_group = queries.shape[1] // key_states.shape[1]
    assert heads == 2 and groups == heads * SIDES and tokens == 2 * BLK
    assert WINDOW == tokens * SIDES * BACK and shards % (2 * SIDES) == 0
    core_at = seq_at % SIDES
    everyone = range(shards)

    def both(array, step, flip):
        pairs = [
            (s * heads + x, (s ^ step) * heads + (x ^ flip)) for s in everyone for x in range(heads)
        ]
        return lax.ppermute(array, ("seq", "head"), pairs)

    def along(array, step):
        pairs = [(s, s + step) for s in everyone if 0 <= s + step < shards]
        return lax.ppermute(array, "seq", pairs)

    def core_swap(array):
        return lax.ppermute(array, "seq", [(s, s ^ 1) for s in everyone])

    def exchange(packets):
        return [
            packets[0],
            both(packets[1], 0, 1),
            both(packets[2], 1, 0),
            both(packets[3], 1, 1),
        ]

    kv_packets = pack(key_states, value_vector_rows, groups)
    qd_packets = pack(queries, grad_output, groups)
    kv_local, qd_packets = lax.optimization_barrier((exchange(kv_packets), qd_packets))
    own = jnp.stack(kv_local)
    qd_local = exchange(qd_packets)
    two_back = along(own, 2 * SIDES)
    one_back = along(own, SIDES)
    three_back = along(own, 3 * SIDES)
    kv_right = key_mover(block_home, kv_local)
    right, left = movers(block_home, qd_local, kv_local)
    right, left, one_back, two_back = lax.optimization_barrier((right, left, one_back, two_back))
    qd_all = qd_local + [along(right, SIDES), along(left, -SIDES)]
    four_back = along(two_back, 2 * SIDES)
    three_back, kv_right = lax.optimization_barrier((three_back, kv_right))
    end_far = along(kv_right, SIDES * (BACK + 1))

    rows = per_group * tokens
    q_width = per_group * HEAD
    pair_shape = jax.ShapeDtypeStruct((SIDES, tokens, 2 * HEAD), jnp.bfloat16)
    kept_shape = jax.ShapeDtypeStruct((tokens, q_width), jnp.bfloat16)
    state = [
        jax.ShapeDtypeStruct((CHUNKS * tokens, 2 * HEAD), jnp.bfloat16),
        jax.ShapeDtypeStruct((CHUNKS, HEAD, tokens), jnp.bfloat16),
        jax.ShapeDtypeStruct((SIDES, CHUNKS - 1, rows, tokens), jnp.bfloat16),
        jax.ShapeDtypeStruct((SIDES, rows, HEAD), jnp.float32),
        jax.ShapeDtypeStruct((SIDES, rows, HEAD), jnp.bfloat16),
        jax.ShapeDtypeStruct((SIDES, rows, HEAD), jnp.bfloat16),
        jax.ShapeDtypeStruct((SIDES, rows, HEAD), jnp.float32),
    ]
    work = 12 * BACK * SIDES * rows * tokens * HEAD
    keep, send, d3, d4, *carried = pl.pallas_call(
        functools.partial(attention_kernel, per_group, tokens, shards),
        out_shape=[kept_shape] * 2 + [pair_shape] * 2 + state,
        in_specs=[SMEM] * 2 + [ANY] * 6 + [VMEM] * 6,
        out_specs=[VMEM] * (4 + len(state)),
        scratch_shapes=[
            pltpu.VMEM((CHUNKS * tokens, 2 * HEAD), jnp.bfloat16),
            pltpu.VMEM((CHUNKS, HEAD, tokens), jnp.bfloat16),
            pltpu.VMEM((SIDES, rows, HEAD), jnp.float32),
            pltpu.VMEM((SIDES, rows, 2 * HEAD), jnp.float32),
            pltpu.VMEM((SIDES, rows, tokens), jnp.bfloat16),
            pltpu.VMEM((2 * SIDES, BLK, 2 * q_width), jnp.bfloat16),
            pltpu.VMEM((BLK, 2 * HEAD), jnp.bfloat16),
            pltpu.SemaphoreType.DMA((2 * SIDES + 1,)),
        ],
        compiler_params=pltpu.CompilerParams(vmem_limit_bytes=34 * 1024 * 1024),
        cost_estimate=pl.CostEstimate(
            flops=work, bytes_accessed=8 * 1024 * 1024, transcendentals=work // (12 * HEAD)
        ),
    )(doc_ids, block_home, *qd_all, own, one_back, two_back, three_back, four_back, end_far)
    dq_keep, dq_send, d0, d1, d2 = pl.pallas_call(
        functools.partial(second_kernel, per_group, tokens),
        out_shape=[kept_shape] * 2 + [pair_shape] * 3,
        in_specs=[SMEM] + [VMEM] * len(state),
        out_specs=[VMEM] * 5,
        scratch_shapes=[
            pltpu.VMEM((SIDES, rows, HEAD), jnp.float32),
            pltpu.VMEM((SIDES, rows, tokens), jnp.bfloat16),
        ],
        compiler_params=pltpu.CompilerParams(vmem_limit_bytes=8 * 1024 * 1024),
        cost_estimate=pl.CostEstimate(
            flops=work, bytes_accessed=8 * 1024 * 1024, transcendentals=0
        ),
    )(doc_ids, *carried)

    def added(term, arrived):
        return term.astype(jnp.float32) + arrived.astype(jnp.float32)

    first_core = core_at == 0

    def halves(pair):
        return (
            jnp.where(first_core, pair[0], pair[1]).astype(jnp.bfloat16),
            jnp.where(first_core, pair[1], pair[0]).astype(jnp.bfloat16),
        )

    four_in = along(d4, -2 * SIDES)
    three_in = along(d3, -SIDES)
    one_in = along(d1, -SIDES)
    own_kept, own_sent = halves(added(d0, one_in))
    own_taken = core_swap(own_sent)
    near_kept, near_sent = halves(added(d2, three_in) + four_in.astype(jnp.float32))
    down = [(s, (s - 2 * SIDES) ^ 1) for s in everyone if s >= 2 * SIDES]
    mine_in = along(near_kept, -2 * SIDES)
    theirs_in = lax.ppermute(near_sent, "seq", down)

    def joined(part):
        kept, taken = part
        return jnp.where(
            first_core,
            jnp.concatenate([kept, taken], axis=1),
            jnp.concatenate([taken, kept], axis=1),
        )

    attended = joined((keep, core_swap(send)))
    grad_query = joined((dq_keep, core_swap(dq_send)))
    mine_in, theirs_in, attended, grad_query = lax.optimization_barrier(
        (mine_in, theirs_in, attended, grad_query)
    )
    mine = added(own_kept, mine_in).astype(jnp.bfloat16)
    theirs = added(own_taken, theirs_in).astype(jnp.bfloat16)
    return (
        attended,
        grad_query,
        joined((mine[:, :HEAD], theirs[:, :HEAD])),
        joined((mine[:, HEAD:], theirs[:, HEAD:])),
    )


def solution(mesh):
    split = P(("seq", "head"), None)
    placed = P("seq", "head")
    return jax.shard_map(
        per_device,
        mesh=mesh,
        in_specs=(split, split, split, split, P(), P()),
        out_specs=(placed, placed, placed, placed),
        check_vma=False,
    )
```

```python
import functools
import math

import jax
import jax.numpy as jnp
from jax import lax
from jax.experimental import pallas as pl
from jax.experimental.pallas import tpu as pltpu
from jax.sharding import PartitionSpec as P

BLK = 128
WINDOW = 2048
HEAD = 128
ROOT = 1.0 / math.sqrt(HEAD)
EXP2_SCALE = ROOT * math.log2(math.e)
HIDDEN = -1e30
NN = (((1,), (0,)), ((), ()))
TN = (((0,), (0,)), ((), ()))
SAFE_TOTAL = 2.0**60
SIDES = 2
BACK = 4
CHUNKS = SIDES * (BACK + 1)
SPLIT = 2 * SIDES
FLIPS = ((0, 0), (0, 1), (1, 0), (1, 1))
VMEM = pl.BlockSpec(memory_space=pltpu.VMEM)
SMEM = pl.BlockSpec(memory_space=pltpu.SMEM)
ANY = pl.BlockSpec(memory_space=pl.ANY)
SMALL = pltpu.CompilerParams(vmem_limit_bytes=8 * 1024 * 1024)
def dot(a, b, dims):
    return lax.dot_general(a, b, dims, preferred_element_type=jnp.float32)


def position():
    seq_at = lax.axis_index("seq")
    return seq_at // SIDES, seq_at % SIDES, lax.axis_index("head")


def local_slots(chip_at, core_at, head_at):
    return [
        SIDES * 2 * chip_at + 2 * (core_at ^ core_flip) + (head_at ^ head_flip)
        for core_flip, head_flip in FLIPS
    ]


def turned(array):
    return jnp.transpose(array.astype(jnp.float32))


def pack_kernel(width, one, two, p0, p1, p2, p3, landed, sems):
    copies = [
        pltpu.make_async_copy(ref, landed.at[which], sems.at[which])
        for which, ref in enumerate((one, two))
    ]
    for copy in copies:
        copy.start()
    for copy in copies:
        copy.wait()
    unused, core_at, head_at = position()
    for target, (core_flip, head_flip) in zip((p0, p1, p2, p3), FLIPS):
        group = SIDES * (head_at ^ head_flip) + (core_at ^ core_flip)
        columns = pl.ds(pl.multiple_of(group * width, width), width)
        for which in range(2):
            target[:, which * width : (which + 1) * width] = landed[which, :, columns]


def pack(one, two, groups):
    rows, columns = one.shape
    width = columns // groups
    packet = jax.ShapeDtypeStruct((rows, 2 * width), jnp.bfloat16)
    return pl.pallas_call(
        functools.partial(pack_kernel, width),
        out_shape=[packet] * 4,
        in_specs=[ANY] * 2,
        out_specs=[VMEM] * 4,
        scratch_shapes=[
            pltpu.VMEM((2, rows, columns), jnp.bfloat16),
            pltpu.SemaphoreType.DMA((2,)),
        ],
        compiler_params=SMALL,
        cost_estimate=pl.CostEstimate(flops=0, bytes_accessed=8 * rows * columns, transcendentals=0),
    )(one, two)


def pack_joined_kernel(width, both, p0, p1, p2, p3):
    unused, core_at, head_at = position()
    total = both.shape[1] // 2
    for target, (core_flip, head_flip) in zip((p0, p1, p2, p3), FLIPS):
        group = SIDES * (head_at ^ head_flip) + (core_at ^ core_flip)
        for which in range(2):
            columns = pl.ds(pl.multiple_of(which * total + group * width, width), width)
            target[:, which * width : (which + 1) * width] = both[:, columns]


def pack_joined(both, groups):
    rows, columns = both.shape
    width = columns // (2 * groups)
    packet = jax.ShapeDtypeStruct((rows, 2 * width), jnp.bfloat16)
    return pl.pallas_call(
        functools.partial(pack_joined_kernel, width),
        out_shape=[packet] * 4,
        in_specs=[VMEM],
        out_specs=[VMEM] * 4,
        compiler_params=SMALL,
        cost_estimate=pl.CostEstimate(flops=0, bytes_accessed=4 * rows * columns, transcendentals=0),
    )(both)


def move_kernel(tables, q0, q1, q2, q3, k0, k1, k2, k3, right, left):
    chip_at, core_at, head_at = position()
    width = q0.shape[1]
    for slot, q, k in zip(local_slots(chip_at, core_at, head_at), (q0, q1, q2, q3), (k0, k1, k2, k3)):
        target = tables[1, slot] // (2 * SIDES)

        @pl.when(target > chip_at)
        def _():
            right[...] = q[...]

        @pl.when(target < chip_at)
        def _():
            left[:, :width] = q[...]
            left[:, width:] = k[...]


def movers(tables, queries, keys):
    rows, width = queries[0].shape
    return pl.pallas_call(
        move_kernel,
        out_shape=[
            jax.ShapeDtypeStruct((rows, width), jnp.bfloat16),
            jax.ShapeDtypeStruct((rows, width + keys[0].shape[1]), jnp.bfloat16),
        ],
        in_specs=[SMEM] + [VMEM] * 8,
        out_specs=[VMEM] * 2,
        compiler_params=SMALL,
        cost_estimate=pl.CostEstimate(flops=0, bytes_accessed=8 * rows * width, transcendentals=0),
    )(tables, *queries, *keys)


def end_kernel(tables, k0, k1, k2, k3, right):
    chip_at, core_at, head_at = position()
    for slot, ref in zip(local_slots(chip_at, core_at, head_at), (k0, k1, k2, k3)):
        @pl.when(tables[1, slot] // (2 * SIDES) > chip_at)
        def _():
            right[...] = ref[...]


def key_mover(tables, keys):
    return pl.pallas_call(
        end_kernel,
        out_shape=jax.ShapeDtypeStruct(keys[0].shape, jnp.bfloat16),
        in_specs=[SMEM] + [VMEM] * 4,
        out_specs=VMEM,
        compiler_params=SMALL,
        cost_estimate=pl.CostEstimate(
            flops=0, bytes_accessed=8 * keys[0].size, transcendentals=0
        ),
    )(tables, *keys)


def block_sources(home, chip_at, core_at, head_at, b):
    slots = local_slots(chip_at, core_at, head_at)
    before = jnp.maximum(2 * SIDES * (chip_at - 1), 0)
    block = 2 * SIDES * chip_at + b
    here = [home[slot] == block for slot in slots]
    from_left = home[before] == block
    for other in range(1, 2 * SIDES):
        from_left = from_left | (home[before + other] == block)
    outside = jnp.logical_not(here[0] | here[1] | here[2] | here[3])
    return here + [outside & from_left, outside & jnp.logical_not(from_left)]


def key_ranges(docs, chip_at):
    first = SIDES * (chip_at - BACK)

    def doc_at(j, half):
        return docs[jnp.maximum(2 * (first + j) + half, 0)]

    limit = [SIDES * BACK + i + 1 for i in range(SIDES)]
    lowest = []
    for i in range(SIDES):
        own = SIDES * BACK + i
        low = jnp.int32(own)
        for j in range(i, own):
            alike = (first + j >= 0) & (doc_at(j, 1) == doc_at(own, 0))
            low = low - alike.astype(jnp.int32)
        lowest.append(low)
    return doc_at, lowest, limit, jnp.minimum(lowest[0], lowest[1])


def gradient_loop(
    per_group, tokens, lowest, limit, start, stop, outputs,
    kv, values_turned, e_low, spread, q_stack, do_stack, dq, ds_low,
):
    def chunk(j):
        return pl.ds(pl.multiple_of(j * tokens, tokens), tokens)

    def store(j, value):
        for back, ref in outputs.items():
            @pl.when(j // SIDES == BACK - back)
            def _():
                ref[j % SIDES] = value

    def grad_terms(i, j):
        value_term = dot(e_low[i, j - i], do_stack[i], TN)
        key_term = None
        for h in range(per_group):
            rows = slice(h * tokens, (h + 1) * tokens)
            delta = spread[i, rows]
            dp = dot(do_stack[i, rows], values_turned[j], NN)
            e = e_low[i, j - i, rows].astype(jnp.float32)
            g0 = e[:, :HEAD] * (dp[:, :HEAD] - delta)
            g1 = e[:, HEAD:] * (dp[:, HEAD:] - delta)
            ds = jnp.concatenate([g0, g1], axis=1).astype(jnp.bfloat16)
            ds_low[i, 0, rows] = ds
            dq[i, rows] += dot(ds, kv[chunk(j), :HEAD], NN)
            if h % 2 == 1:
                part = slice((h - 1) * tokens, (h + 1) * tokens)
                term = dot(ds_low[i, 0, part], q_stack[i, part], TN)
                key_term = term if key_term is None else key_term + term
        return jnp.concatenate([key_term * ROOT, value_term], axis=1)

    def grad_pass(j, carry):
        inside = [(j >= lowest[i]) & (j < limit[i]) for i in range(SIDES)]

        @pl.when(inside[0] & inside[1])
        def _():
            store(j, (grad_terms(0, j) + grad_terms(1, j)).astype(jnp.bfloat16))

        for i in range(SIDES):
            @pl.when(inside[i] & jnp.logical_not(inside[1 - i]))
            def _():
                store(j, grad_terms(i, j).astype(jnp.bfloat16))

        return carry

    def two_terms(i, j):
        value_terms = [dot(e_low[i, j + step - i], do_stack[i], TN) for step in range(2)]
        key_terms = [None, None]
        for h in range(per_group):
            rows = slice(h * tokens, (h + 1) * tokens)
            delta = spread[i, rows]
            parts = []
            for step in range(2):
                dp = dot(do_stack[i, rows], values_turned[j + step], NN)
                e = e_low[i, j + step - i, rows].astype(jnp.float32)
                g0 = e[:, :HEAD] * (dp[:, :HEAD] - delta)
                g1 = e[:, HEAD:] * (dp[:, HEAD:] - delta)
                ds = jnp.concatenate([g0, g1], axis=1).astype(jnp.bfloat16)
                ds_low[i, step, rows] = ds
                parts.append(ds)
            keys = kv[pl.ds(pl.multiple_of(j * tokens, tokens), 2 * tokens), :HEAD]
            dq[i, rows] += dot(jnp.concatenate(parts, axis=1), keys, NN)
            if h % 2 == 1:
                part = slice((h - 1) * tokens, (h + 1) * tokens)
                for step in range(2):
                    term = dot(ds_low[i, step, part], q_stack[i, part], TN)
                    before = key_terms[step]
                    key_terms[step] = term if before is None else before + term
        return [
            jnp.concatenate([key_terms[step] * ROOT, value_terms[step]], axis=1)
            for step in range(2)
        ]

    def no_terms(j, carry):
        store(j, jnp.zeros((tokens, 2 * HEAD), jnp.bfloat16))
        return carry

    def seen_by_both(j):
        return (j >= lowest[0]) & (j >= lowest[1]) & (j < limit[0])

    def two_pass(t, carry):
        j = start + 2 * t
        whole = seen_by_both(j) & seen_by_both(j + 1)

        @pl.when(whole)
        def _():
            sums = [first + second for first, second in zip(two_terms(0, j), two_terms(1, j))]
            for step in range(2):
                store(j + step, sums[step].astype(jnp.bfloat16))

        @pl.when(jnp.logical_not(whole))
        def _():
            begin = jnp.clip(jnp.minimum(lowest[0], lowest[1]), j, j + 2)
            lax.fori_loop(j, begin, no_terms, 0)
            lax.fori_loop(begin, j + 2, grad_pass, 0)

        return carry

    lax.fori_loop(0, (stop - start) // 2, two_pass, 0)


def attention_kernel(
    per_group, tokens, shards,
    tables, b0, b1, b2, b3, b4, b5, c0, c1, c2, c3, c4, end_far,
    keep, send, d3, d4, kv, values_turned, e_low, spread, q_stack, do_stack, dq,
    ones, keys_turned, top, acc, ds_low, landed, end_near, sems,
):
    chip_at, core_at, head_at = position()
    q_width = per_group * HEAD
    docs, home = tables.at[0], tables.at[1]

    def land(ref, b):
        return pltpu.make_async_copy(ref.at[:, pl.ds(0, 2 * q_width)], landed.at[b], sems.at[b])

    end_copy = pltpu.make_async_copy(
        b5.at[:, pl.ds(2 * q_width, 2 * HEAD)], end_near, sems.at[2 * SIDES]
    )
    end_copy.start()

    for b in range(2 * SIDES):
        flags = block_sources(home, chip_at, core_at, head_at, b)
        for flag, ref in zip(flags, (b0, b1, b2, b3, b4, b5)):
            @pl.when(flag)
            def _():
                land(ref, b).start()

    chip_blocks = 2 * SIDES
    window = chip_blocks * (chip_at - BACK)

    def write_key_block(block, known, value):
        place = block - window

        @pl.when(known & (place >= 0) & (place < chip_blocks * (BACK + 1)))
        def _():
            rows = pl.ds(pl.multiple_of(place * BLK, BLK), BLK)
            kv[rows] = value[...]
            ones[rows, :HEAD] = value[:, HEAD:]
            ones[rows, HEAD:] = jnp.ones((BLK, HEAD), jnp.bfloat16)

    def write_chip(back, ref):
        known = chip_at >= back
        for which, slot in enumerate(local_slots(chip_at - back, core_at, head_at)):
            write_key_block(home[jnp.maximum(slot, 0)], known, ref.at[which])

    def write_end(chip, target, ref):
        known = (chip >= 0) & (chip < shards // SIDES)
        slot = jnp.where(known, chip_blocks * chip, 0)
        for other in range(chip_blocks):
            block = home[slot + other]
            write_key_block(block, known & (block // chip_blocks == target), ref)

    for back, ref in enumerate((c0, c1, c2, c3, c4)):
        write_chip(back, ref)
    write_end(chip_at - BACK - 1, chip_at - BACK, end_far)
    end_copy.wait()
    write_end(chip_at + 1, chip_at, end_near)
    for b in range(2 * SIDES):
        land(b0, b).wait()
        for h in range(per_group):
            rows = slice(h * tokens + (b % 2) * BLK, h * tokens + (b % 2 + 1) * BLK)
            q_stack[b // 2, rows] = landed[b, :, h * HEAD : (h + 1) * HEAD]
            do_stack[b // 2, rows] = landed[b, :, q_width + h * HEAD : q_width + (h + 1) * HEAD]

    def chunk(j):
        return pl.ds(pl.multiple_of(j * tokens, tokens), tokens)

    doc_at, lowest, limit, begin = key_ranges(docs, chip_at)

    row = lax.broadcasted_iota(jnp.int32, (tokens, tokens), 0)
    col = lax.broadcasted_iota(jnp.int32, (tokens, tokens), 1)

    def hidden(i, j):
        own = SIDES * BACK + i
        q_doc = jnp.where(row < BLK, doc_at(own, 0), doc_at(own, 1))
        k_doc = jnp.where(col < BLK, doc_at(j, 0), doc_at(j, 1))
        gap = row - col + (own - j) * tokens
        seen = (q_doc == k_doc) & (gap >= 0) & (gap < WINDOW)
        return jnp.where(seen, 0.0, HIDDEN)

    k_cols = slice(0, HEAD)
    v_cols = slice(HEAD, 2 * HEAD)

    def turn_chunk(j, carry):
        keys_turned[j] = turned(kv[chunk(j), k_cols]).astype(jnp.bfloat16)
        values_turned[j] = turned(kv[chunk(j), v_cols]).astype(jnp.bfloat16)
        return carry

    lax.fori_loop(begin, CHUNKS, turn_chunk, 0)

    def head_rows(h):
        return slice(h * tokens, (h + 1) * tokens)

    def in_range(i, j):
        return (j >= lowest[i]) & (j < limit[i])

    def is_open(i, j):
        own = SIDES * BACK + i
        return (
            in_range(i, j)
            & (doc_at(j, 0) == doc_at(own, 1))
            & (j < own)
            & (j > own - SIDES * BACK)
        )

    def take_top(i, start):
        top[i] = jnp.full_like(top[i], HIDDEN)

        def widen(j, carry):
            bias = hidden(i, j)
            for h in range(per_group):
                rows = head_rows(h)
                s = dot(q_stack[i, rows], keys_turned[j], NN) + bias
                top[i, rows] = jnp.maximum(top[i, rows], jnp.maximum(s[:, :HEAD], s[:, HEAD:]))
            return carry

        lax.fori_loop(start, limit[i], widen, 0)
        for h in range(per_group):
            rows = head_rows(h)
            top[i, rows] = jnp.broadcast_to(
                jnp.max(top[i, rows], axis=1, keepdims=True), (tokens, HEAD)
            )

    def forward(i, j, bias):
        for h in range(per_group):
            rows = head_rows(h)
            s = dot(q_stack[i, rows], keys_turned[j], NN)
            if bias is not None:
                s = s + bias
            m = top[i, rows]
            e0 = jnp.exp2((s[:, :HEAD] - m) * EXP2_SCALE)
            e1 = jnp.exp2((s[:, HEAD:] - m) * EXP2_SCALE)
            low = jnp.concatenate([e0, e1], axis=1).astype(jnp.bfloat16)
            e_low[i, j - i, rows] = low
            acc[i, rows] += dot(low, ones[chunk(j)], NN)

    def forward_two(i, j):
        for h in range(per_group):
            rows = head_rows(h)
            m = top[i, rows]
            lows = []
            for step in range(2):
                s = dot(q_stack[i, rows], keys_turned[j + step], NN)
                e0 = jnp.exp2((s[:, :HEAD] - m) * EXP2_SCALE)
                e1 = jnp.exp2((s[:, HEAD:] - m) * EXP2_SCALE)
                low = jnp.concatenate([e0, e1], axis=1).astype(jnp.bfloat16)
                e_low[i, j + step - i, rows] = low
                lows.append(low)
            values = ones[pl.ds(pl.multiple_of(j * tokens, tokens), 2 * tokens)]
            acc[i, rows] += dot(jnp.concatenate(lows, axis=1), values, NN)

    last_open = SIDES * BACK
    open_count = jnp.int32(0)
    for j in range(SIDES * BACK):
        open_count = open_count + (is_open(0, j) & is_open(1, j)).astype(jnp.int32)
    twos = open_count // 2

    def two_pass(t, carry):
        for i in range(SIDES):
            forward_two(i, last_open - 2 * (t + 1))
        return carry

    def other_pass(t, carry):
        return forward_pass(jnp.where(t < last_open - 2 * twos, t, t + 2 * twos), carry)

    def forward_pass(j, carry):
        open_all = is_open(0, j) & is_open(1, j)

        @pl.when(open_all)
        def _():
            for i in range(SIDES):
                forward(i, j, None)

        for i in range(SIDES):
            @pl.when(in_range(i, j) & jnp.logical_not(open_all))
            def _():
                forward(i, j, hidden(i, j))

        return carry

    def attempt(carry):
        tries, unused = carry
        for i in range(SIDES):
            take_top(i, jnp.where(tries == 0, SIDES * BACK + i, lowest[i]))
        acc[...] = jnp.zeros_like(acc)
        lax.fori_loop(0, twos, two_pass, 0)
        lax.fori_loop(begin, CHUNKS - 2 * twos, other_pass, 0)
        safe = jnp.min(jnp.where(acc[:, :, HEAD:] < SAFE_TOTAL, 1.0, 0.0))
        return tries + 1, (safe < 0.5).astype(jnp.int32)

    lax.while_loop(
        lambda carry: (carry[0] == 0) | ((carry[0] == 1) & (carry[1] == 1)),
        attempt,
        (jnp.int32(0), jnp.int32(0)),
    )

    for i in range(SIDES):
        for h in range(per_group):
            rows = head_rows(h)
            inverse = 1.0 / acc[i, rows, HEAD:]
            attended = (acc[i, rows, :HEAD] * inverse).astype(jnp.bfloat16)

            @pl.when(core_at == i)
            def _():
                keep[:, h * HEAD : (h + 1) * HEAD] = attended

            @pl.when(core_at != i)
            def _():
                send[:, h * HEAD : (h + 1) * HEAD] = attended

            shared = (do_stack[i, rows].astype(jnp.float32) * inverse).astype(jnp.bfloat16)
            do_stack[i, rows] = shared
            delta = jnp.sum(
                shared.astype(jnp.float32) * attended.astype(jnp.float32), axis=1, keepdims=True
            )
            spread[i, rows] = jnp.broadcast_to(delta, (tokens, HEAD))
    dq[...] = jnp.zeros_like(dq)

    gradient_loop(
        per_group, tokens, lowest, limit, 0, SPLIT, {3: d3, 4: d4},
        kv, values_turned, e_low, spread, q_stack, do_stack, dq, ds_low,
    )


def second_kernel(
    per_group, tokens,
    tables, kv, values_turned, e_low, spread, q_stack, do_stack, dq_first,
    keep, send, d0, d1, d2, dq, ds_low,
):
    chip_at, core_at, head_at = position()
    unused, lowest, limit, begin = key_ranges(tables.at[0], chip_at)
    dq[...] = dq_first[...]
    gradient_loop(
        per_group, tokens, lowest, limit, SPLIT, CHUNKS, {0: d0, 1: d1, 2: d2},
        kv, values_turned, e_low, spread, q_stack, do_stack, dq, ds_low,
    )
    for i in range(SIDES):
        for h in range(per_group):
            gradient = (dq[i, h * tokens : (h + 1) * tokens] * ROOT).astype(jnp.bfloat16)

            @pl.when(core_at == i)
            def _():
                keep[:, h * HEAD : (h + 1) * HEAD] = gradient

            @pl.when(core_at != i)
            def _():
                send[:, h * HEAD : (h + 1) * HEAD] = gradient


def per_device(queries, key_states, value_vector_rows, grad_output, doc_ids, block_home):
    seq_at = lax.axis_index("seq")
    shards = lax.axis_size("seq")
    heads = lax.axis_size("head")
    tokens = queries.shape[0] * heads
    groups = key_states.shape[1] // HEAD
    per_group = queries.shape[1] // key_states.shape[1]
    assert heads == 2 and groups == heads * SIDES and tokens == 2 * BLK
    assert WINDOW == tokens * SIDES * BACK and shards % (2 * SIDES) == 0
    core_at = seq_at % SIDES
    everyone = range(shards)

    def both(array, step, flip):
        pairs = [
            (s * heads + x, (s ^ step) * heads + (x ^ flip)) for s in everyone for x in range(heads)
        ]
        return lax.ppermute(array, ("seq", "head"), pairs)

    def along(array, step):
        pairs = [(s, s + step) for s in everyone if 0 <= s + step < shards]
        return lax.ppermute(array, "seq", pairs)

    def core_swap(array):
        return lax.ppermute(array, "seq", [(s, s ^ 1) for s in everyone])

    def exchange(packets):
        return [
            packets[0],
            both(packets[1], 0, 1),
            both(packets[2], 1, 0),
            both(packets[3], 1, 1),
        ]

    tables = jnp.stack([doc_ids, block_home])
    kv_packets = pack_joined(
        jnp.concatenate([key_states, value_vector_rows], axis=1), groups
    )
    qd_packets = pack(queries, grad_output, groups)
    kv_local, qd_packets = lax.optimization_barrier((exchange(kv_packets), qd_packets))
    own = jnp.stack(kv_local)
    qd_local = exchange(qd_packets)
    two_back = along(own, 2 * SIDES)
    one_back = along(own, SIDES)
    three_back = along(own, 3 * SIDES)
    kv_right = key_mover(tables, kv_local)
    right, left = movers(tables, qd_local, kv_local)
    right, left, two_back = lax.optimization_barrier((right, left, two_back))
    qd_all = qd_local + [along(right, SIDES), along(left, -SIDES)]
    four_back = along(two_back, 2 * SIDES)
    one_back, three_back, kv_right = lax.optimization_barrier((one_back, three_back, kv_right))
    end_far = along(kv_right, SIDES * (BACK + 1))

    rows = per_group * tokens
    q_width = per_group * HEAD
    pair_shape = jax.ShapeDtypeStruct((SIDES, tokens, 2 * HEAD), jnp.bfloat16)
    kept_shape = jax.ShapeDtypeStruct((tokens, q_width), jnp.bfloat16)
    state = [
        jax.ShapeDtypeStruct((CHUNKS * tokens, 2 * HEAD), jnp.bfloat16),
        jax.ShapeDtypeStruct((CHUNKS, HEAD, tokens), jnp.bfloat16),
        jax.ShapeDtypeStruct((SIDES, CHUNKS - 1, rows, tokens), jnp.bfloat16),
        jax.ShapeDtypeStruct((SIDES, rows, HEAD), jnp.float32),
        jax.ShapeDtypeStruct((SIDES, rows, HEAD), jnp.bfloat16),
        jax.ShapeDtypeStruct((SIDES, rows, HEAD), jnp.bfloat16),
        jax.ShapeDtypeStruct((SIDES, rows, HEAD), jnp.float32),
    ]
    work = 12 * BACK * SIDES * rows * tokens * HEAD
    keep, send, d3, d4, *carried = pl.pallas_call(
        functools.partial(attention_kernel, per_group, tokens, shards),
        out_shape=[kept_shape] * 2 + [pair_shape] * 2 + state,
        in_specs=[SMEM] + [ANY] * 6 + [VMEM] * 6,
        out_specs=[VMEM] * (4 + len(state)),
        scratch_shapes=[
            pltpu.VMEM((CHUNKS * tokens, 2 * HEAD), jnp.bfloat16),
            pltpu.VMEM((CHUNKS, HEAD, tokens), jnp.bfloat16),
            pltpu.VMEM((SIDES, rows, HEAD), jnp.float32),
            pltpu.VMEM((SIDES, rows, 2 * HEAD), jnp.float32),
            pltpu.VMEM((SIDES, 2, rows, tokens), jnp.bfloat16),
            pltpu.VMEM((2 * SIDES, BLK, 2 * q_width), jnp.bfloat16),
            pltpu.VMEM((BLK, 2 * HEAD), jnp.bfloat16),
            pltpu.SemaphoreType.DMA((2 * SIDES + 1,)),
        ],
        compiler_params=pltpu.CompilerParams(vmem_limit_bytes=34 * 1024 * 1024),
        cost_estimate=pl.CostEstimate(
            flops=work, bytes_accessed=8 * 1024 * 1024, transcendentals=work // (12 * HEAD)
        ),
    )(tables, *qd_all, own, one_back, two_back, three_back, four_back, end_far)
    dq_keep, dq_send, d0, d1, d2 = pl.pallas_call(
        functools.partial(second_kernel, per_group, tokens),
        out_shape=[kept_shape] * 2 + [pair_shape] * 3,
        in_specs=[SMEM] + [VMEM] * len(state),
        out_specs=[VMEM] * 5,
        scratch_shapes=[
            pltpu.VMEM((SIDES, rows, HEAD), jnp.float32),
            pltpu.VMEM((SIDES, 2, rows, tokens), jnp.bfloat16),
        ],
        compiler_params=pltpu.CompilerParams(vmem_limit_bytes=8 * 1024 * 1024),
        cost_estimate=pl.CostEstimate(
            flops=work, bytes_accessed=8 * 1024 * 1024, transcendentals=0
        ),
    )(tables, *carried)

    def added(term, arrived):
        return term.astype(jnp.float32) + arrived.astype(jnp.float32)

    first_core = core_at == 0

    def halves(pair):
        return (
            jnp.where(first_core, pair[0], pair[1]).astype(jnp.bfloat16),
            jnp.where(first_core, pair[1], pair[0]).astype(jnp.bfloat16),
        )

    four_in = along(d4, -2 * SIDES)
    three_in = along(d3, -SIDES)
    one_in = along(d1, -SIDES)
    own_kept, own_sent = halves(added(d0, one_in))
    own_taken = core_swap(own_sent)
    near_kept, near_sent = halves(added(d2, three_in) + four_in.astype(jnp.float32))
    down = [(s, (s - 2 * SIDES) ^ 1) for s in everyone if s >= 2 * SIDES]
    mine_in = along(near_kept, -2 * SIDES)
    theirs_in = lax.ppermute(near_sent, "seq", down)

    def joined(part):
        kept, taken = part
        return jnp.where(
            first_core,
            jnp.concatenate([kept, taken], axis=1),
            jnp.concatenate([taken, kept], axis=1),
        )

    attended = joined((keep, core_swap(send)))
    grad_query = joined((dq_keep, core_swap(dq_send)))
    mine_in, theirs_in, attended, grad_query = lax.optimization_barrier(
        (mine_in, theirs_in, attended, grad_query)
    )
    mine = added(own_kept, mine_in).astype(jnp.bfloat16)
    theirs = added(own_taken, theirs_in).astype(jnp.bfloat16)
    return (
        attended,
        grad_query,
        joined((mine[:, :HEAD], theirs[:, :HEAD])),
        joined((mine[:, HEAD:], theirs[:, HEAD:])),
    )


def solution(mesh):
    split = P(("seq", "head"), None)
    placed = P("seq", "head")
    return jax.shard_map(
        per_device,
        mesh=mesh,
        in_specs=(split, split, split, split, P(), P()),
        out_specs=(placed, placed, placed, placed),
        check_vma=False,
    )
```
